32 devices in a mesh: chan: 16 (over z, y, core), freq: 2 (over x).
Axes of the slice: x: 2, y: 2, z: 4, core: 2. Of those that a mesh axis runs over, the one named last changes fastest.
Arguments:
- records: bfloat16 [2048, 64, 512], P('chan', 'freq'), may hold values from -6 to 6
- taper_select: int32 [64], P('freq'), may hold values from 0 to 3
- source_index: int32 [128], replicated, may hold values from 0 to 2047
Outputs:
- correlations: bfloat16 [2048, 128, 256], P('chan', 'freq')
The draws below stay inside these ranges and needn't reach their ends.
Inputs may be any that keep to these rules, and one draw needn't show every extreme that they name: `source_index`: sources may repeat.
All inputs are finite; a program needn't handle non-finite values.
Results may differ from the reference program's by a relative error of at most 0.0082.
Values may be sent and summed in bfloat16 or wider, within the bound.
A program may use at most 128 MiB of HBM per device.

```python
import math
import jax
import jax.numpy as jnp
from jax import lax

CH_DEV = 128
NWIN = 512
NFREQ = 256
NSRC = 128
LAGS = 256
NCH = 2048
SEGS = 64


def touch_ends(result, key, least, top_value):
    extent = result.shape
    spot = [jax.random.randint(jax.random.fold_in(key, axis), (), 0, extent[axis]) for axis in range(len(extent))]
    result = result.at[tuple(spot)].set(least)
    longest = extent.index(max(extent))
    spot[longest] = (spot[longest] + 1) % extent[longest]
    return result.at[tuple(spot)].set(top_value)


def level_of(rng, shape, shards, low, high):
    level = 1.0
    for axis_at, blocks in shards:
        steps = jax.random.uniform(jax.random.fold_in(jax.random.fold_in(rng, 6), axis_at), (blocks,), jnp.float32, low / len(shards), high / len(shards))
        level = level * jnp.repeat(jnp.exp(steps), shape[axis_at] // blocks).reshape((-1,) + (1,) * (len(shape) - 1 - axis_at))
    return level


def bell_draw(rng, extent, width, most, cuts=(), held_as=jnp.bfloat16):
    gain = level_of(rng, extent, cuts, -0.22, 0.18) if cuts else 1.0
    values = jax.random.normal(rng, extent, jnp.float32) * width * gain
    return jnp.minimum(jnp.maximum(values, -most), most).astype(held_as)


def setup_inputs(seed: int = 0) -> dict:
    splits = jax.random.split(jax.random.key(seed), 4)
    records = bell_draw(splits[0], (NCH, SEGS, NWIN), 1.0, 6.0, ((0, 16), (1, 2)))
    taper_select = touch_ends(jax.random.randint(splits[1], (SEGS,), 0, 4), jax.random.fold_in(splits[1], 1), 0, 3).astype(jnp.int32)
    source_index = touch_ends(jax.random.randint(splits[2], (NSRC,), 0, NCH), jax.random.fold_in(splits[2], 1), 0, NCH - 1).astype(jnp.int32)
    return dict(records=records, taper_select=taper_select, source_index=source_index)


def make_tables(nwin, nfreq, lags):
    n_int = jnp.arange(nwin, dtype=jnp.int32)
    k_int = jnp.arange(nfreq, dtype=jnp.int32)
    phase = (n_int[:, None] * k_int[None, :] % nwin).astype(jnp.float32) * (2.0 * math.pi / nwin)
    dft_table = (jnp.concatenate([jnp.cos(phase), -jnp.sin(phase)], axis=1) / math.sqrt(nwin)).astype(jnp.bfloat16)
    sine = jnp.sin(math.pi * (n_int.astype(jnp.float32) + 0.5) / nwin)
    powers = jnp.array([0.5, 1.0, 2.0, 3.0], jnp.float32)
    taper_table = jnp.power(sine[None, :], powers[:, None])
    half = nfreq // 4
    gap = jnp.abs(k_int[:, None] - k_int[None, :])
    band = (gap <= half).astype(jnp.float32)
    lag_int = jnp.arange(lags, dtype=jnp.int32) - lags // 2
    lphase = (k_int[:, None] * lag_int[None, :] % nwin).astype(jnp.float32) * (2.0 * math.pi / nwin)
    weight = jnp.where(k_int == 0, 1.0, 2.0).astype(jnp.float32)[:, None] / math.sqrt(2.0 * nfreq)
    inverse_table = jnp.concatenate([weight * jnp.cos(lphase), -weight * jnp.sin(lphase)], axis=0).astype(jnp.bfloat16)
    return (dft_table, taper_table, band, inverse_table, 2 * half + 1)

def whiten(block, taper, dft_table, band, count):
    chans, segs, nwin = block.shape
    nfreq = nwin // 2
    tapered = (block.astype(jnp.float32) * taper[None, :, :]).astype(jnp.bfloat16)
    spectra = jnp.dot(tapered.reshape(chans * segs, nwin), dft_table, preferred_element_type=jnp.float32)
    real_part = spectra[:, :nfreq]
    imag_part = spectra[:, nfreq:]
    power = real_part * real_part + imag_part * imag_part
    smooth = jnp.dot(power, band, precision=lax.Precision.HIGHEST) / count
    factor = 1.0 / jnp.sqrt(smooth + 1e-06)
    whitened = jnp.stack([real_part * factor, imag_part * factor], axis=1).astype(jnp.bfloat16)
    return whitened.reshape(chans, segs, 2, nfreq)

def cross_spectra(receivers, sources, segs):
    real_r = receivers[:, :, 0, :].astype(jnp.float32)
    imag_r = receivers[:, :, 1, :].astype(jnp.float32)
    real_s = sources[:, :, 0, :].astype(jnp.float32)
    imag_s = sources[:, :, 1, :].astype(jnp.float32)
    real_c = jnp.einsum('cgf,sgf->csf', real_r, real_s) + jnp.einsum('cgf,sgf->csf', imag_r, imag_s)
    imag_c = jnp.einsum('cgf,sgf->csf', imag_r, real_s) - jnp.einsum('cgf,sgf->csf', real_r, imag_s)
    return (jnp.stack([real_c, imag_c], axis=2) / math.sqrt(segs)).astype(jnp.bfloat16)

def reference(records, taper_select, source_index):
    dft_table, taper_table, band, inverse_table, count = make_tables(NWIN, NFREQ, LAGS)
    taper = taper_table[taper_select]
    sources = whiten(records[source_index], taper, dft_table, band, count)
    blocks = records.reshape(NCH // CH_DEV, CH_DEV, SEGS, NWIN)

    def one_block(block):
        whitened = whiten(block, taper, dft_table, band, count)
        cross = cross_spectra(whitened, sources, SEGS)
        flat = cross.reshape(CH_DEV * NSRC, 2 * NFREQ)
        lagged = jnp.dot(flat, inverse_table, preferred_element_type=jnp.float32)
        return lagged.astype(jnp.bfloat16).reshape(CH_DEV, NSRC, LAGS)
    return lax.map(one_block, blocks).reshape(NCH, NSRC, LAGS)
```

```python
import functools
import math

import jax
import jax.numpy as jnp
import ml_dtypes
import numpy as np
from jax import lax
from jax.experimental import pallas as pl
from jax.experimental.pallas import tpu as pltpu
from jax.sharding import PartitionSpec as P

LAGS = 256
STEP = 16
F32 = jnp.float32
BF16 = jnp.bfloat16


def make_tables(nwin, nfreq, lags):
    n_int = np.arange(nwin)
    k_int = np.arange(nfreq)
    phase = (n_int[:, None] * k_int[None, :] % nwin) * (2.0 * math.pi / nwin)
    dft = np.concatenate([np.cos(phase), -np.sin(phase)], axis=1) / math.sqrt(nwin)
    sine = np.sin(math.pi * (n_int + 0.5) / nwin)
    taper = np.power(sine[None, :], np.array([0.5, 1.0, 2.0, 3.0])[:, None])
    half = nfreq // 4
    band = np.abs(k_int[:, None] - k_int[None, :]) <= half
    lag_int = np.arange(lags) - lags // 2
    lphase = (k_int[:, None] * lag_int[None, :] % nwin) * (2.0 * math.pi / nwin)
    weight = np.where(k_int == 0, 1.0, 2.0)[:, None] / math.sqrt(2.0 * nfreq)
    inverse = np.concatenate([weight * np.cos(lphase), -weight * np.sin(lphase)], axis=0)
    low = ml_dtypes.bfloat16
    return (
        dft.T.astype(np.float32).astype(low),
        taper.astype(np.float32),
        band.astype(low),
        inverse.T.astype(np.float32).astype(low),
        2 * half + 1,
    )


def pick_kernel(owned_ref, row_ref, x_ref, o_ref):
    def one(s, carry):
        keep = jnp.where(owned_ref[s] == 1, 1.0, 0.0).astype(BF16)
        o_ref[s] = x_ref[row_ref[s]] * keep
        return carry

    lax.fori_loop(0, o_ref.shape[0], one, 0)


def pick(records, owned, rows):
    count = rows.shape[0]
    smem = pl.BlockSpec(memory_space=pltpu.SMEM)
    vmem = pl.BlockSpec(memory_space=pltpu.VMEM)
    return pl.pallas_call(
        pick_kernel,
        out_shape=jax.ShapeDtypeStruct((count,) + records.shape[1:], BF16),
        in_specs=[smem, smem, vmem],
        out_specs=vmem,
        compiler_params=pltpu.CompilerParams(vmem_limit_bytes=40 << 20),
        name="pick",
    )(owned, rows, records)


def whiten_kernel(count, x_ref, t_ref, dft_ref, band_ref, o_ref, xf, of):
    chans, segs, nwin = x_ref.shape
    nfreq = nwin // 2
    lane = 128
    for q in range(nwin // lane):
        cols = slice(q * lane, (q + 1) * lane)
        x = x_ref[:, :, cols].astype(F32) * t_ref[:, cols][None]
        xf[q] = x.reshape(chans * segs, lane)
    for p in range(segs // 2):
        pair = []
        for g in (2 * p, 2 * p + 1):
            parts = [xf[q, pl.ds(g, chans, stride=segs), :] for q in range(nwin // lane)]
            pair.append(jnp.concatenate(parts, axis=1).astype(BF16))
        both = jnp.concatenate(pair, axis=0)
        spectra = lax.dot_general(
            dft_ref[...], both, (((1,), (1,)), ((), ())), preferred_element_type=F32
        )
        real, imag = spectra[:nfreq], spectra[nfreq:]
        power = real * real + imag * imag
        high = power.astype(BF16)
        low = (power - high.astype(F32)).astype(BF16)
        smooth = jnp.dot(band_ref[...], high, preferred_element_type=F32)
        smooth += jnp.dot(band_ref[...], low, preferred_element_type=F32)
        factor = lax.rsqrt(smooth * (1.0 / count) + 1e-06)
        real, imag = real * factor, imag * factor
        for j in range(2):
            cols = slice(j * chans, (j + 1) * chans)
            of[pl.ds(2 * p + j, nfreq, stride=2 * segs), :] = real[:, cols]
            of[pl.ds(segs + 2 * p + j, nfreq, stride=2 * segs), :] = imag[:, cols]
    o_ref[...] = of[...].reshape(nfreq, 2, segs, chans).astype(BF16)


def whiten_across(records, taper, dft, band, count):
    chans, segs, nwin = records.shape
    nfreq = nwin // 2
    return pl.pallas_call(
        functools.partial(whiten_kernel, count),
        out_shape=jax.ShapeDtypeStruct((nfreq, 2, segs, chans), BF16),
        grid=(segs // STEP,),
        in_specs=[
            pl.BlockSpec((chans, STEP, nwin), lambda i: (0, i, 0)),
            pl.BlockSpec((STEP, nwin), lambda i: (i, 0)),
            pl.BlockSpec((nwin, nwin), lambda i: (0, 0)),
            pl.BlockSpec((nfreq, nfreq), lambda i: (0, 0)),
        ],
        out_specs=pl.BlockSpec((nfreq, 2, STEP, chans), lambda i: (0, 0, i, 0)),
        scratch_shapes=[
            pltpu.VMEM((nwin // 128, chans * STEP, 128), F32),
            pltpu.VMEM((nfreq * 2 * STEP, chans), F32),
        ],
        compiler_params=pltpu.CompilerParams(vmem_limit_bytes=48 << 20),
        cost_estimate=pl.CostEstimate(
            flops=4 * chans * segs * nwin * nwin,
            bytes_accessed=4 * chans * segs * nwin,
            transcendentals=0,
        ),
        name="whiten_across",
    )(records, taper, dft, band)


def whiten_rows(block, taper, dft, band, count):
    nfreq = block.shape[-1] // 2
    tapered = (block.astype(F32) * taper).astype(BF16)
    spectra = lax.dot_general(
        tapered, dft, (((tapered.ndim - 1,), (1,)), ((), ())), preferred_element_type=F32
    )
    real, imag = spectra[..., :nfreq], spectra[..., nfreq:]
    power = real * real + imag * imag
    high = power.astype(BF16)
    low = (power - high.astype(F32)).astype(BF16)
    smooth = jnp.dot(high, band, preferred_element_type=F32)
    smooth += jnp.dot(low, band, preferred_element_type=F32)
    factor = lax.rsqrt(smooth / count + 1e-06)
    return jnp.stack([real * factor, imag * factor], axis=-2).astype(BF16)


def cross_kernel(nf, scale, *refs):
    *r_refs, s_ref, inv_ref, o_ref, zs, os = refs
    fb, srcs, depth = s_ref.shape
    nfreq2 = inv_ref.shape[1]
    nfreq = nfreq2 // 2
    chans, group, lags = o_ref.shape
    half = depth // 2
    step = pl.program_id(0)

    @pl.when(step < nf)
    def _():
        for j in range(fb):
            parts = []
            for part in range(2):
                for r in r_refs:
                    parts.append(r[j, part])
            receivers = jnp.concatenate(parts, axis=0)
            s = s_ref[j]
            turned = jnp.concatenate([-s[:, half:], s[:, :half]], axis=1)
            both = jnp.concatenate([s, turned], axis=0)
            cross = jnp.dot(both, receivers, preferred_element_type=F32) * scale
            f = step * fb + j
            zs[pl.ds(f, srcs, stride=nfreq2), :] = cross[:srcs]
            zs[pl.ds(nfreq + f, srcs, stride=nfreq2), :] = cross[srcs:]

    @pl.when(step >= nf)
    def _():
        first = (step - nf) * group
        for p in range(group // 2):
            pair = []
            for t in (2 * p, 2 * p + 1):
                row = pl.multiple_of((first + t) * nfreq2, nfreq2)
                pair.append(zs[pl.ds(row, nfreq2), :].astype(BF16))
            lagged = jnp.dot(
                inv_ref[...], jnp.concatenate(pair, axis=1), preferred_element_type=F32
            )
            turned = lagged.T
            for t in range(2):
                for q in range(lags // 128):
                    os[q, pl.ds(2 * p + t, chans, stride=group), :] = turned[
                        t * chans : (t + 1) * chans, q * 128 : (q + 1) * 128
                    ]
        for q in range(lags // 128):
            o_ref[:, :, q * 128 : (q + 1) * 128] = (
                os[q].reshape(chans, group, 128).astype(BF16)
            )


def cross_lags(receivers, sources, inverse, scale):
    nfreq, srcs, depth = sources.shape
    chans = receivers[0].shape[-1]
    lags = inverse.shape[0]
    fb = 16
    nf = nfreq // fb
    group = min(16, srcs)
    ns = srcs // group
    r_specs = [
        pl.BlockSpec((fb,) + r.shape[1:], lambda i: (jnp.minimum(i, nf - 1), 0, 0, 0))
        for r in receivers
    ]
    return pl.pallas_call(
        functools.partial(cross_kernel, nf, scale),
        out_shape=jax.ShapeDtypeStruct((chans, srcs, lags), BF16),
        grid=(nf + ns,),
        in_specs=r_specs
        + [
            pl.BlockSpec((fb, srcs, depth), lambda i: (jnp.minimum(i, nf - 1), 0, 0)),
            pl.BlockSpec(inverse.shape, lambda i: (0, 0)),
        ],
        out_specs=pl.BlockSpec((chans, group, lags), lambda i: (0, jnp.maximum(i - nf, 0), 0)),
        scratch_shapes=[
            pltpu.VMEM((srcs * 2 * nfreq, chans), F32),
            pltpu.VMEM((lags // 128, chans * group, 128), F32),
        ],
        compiler_params=pltpu.CompilerParams(vmem_limit_bytes=56 << 20),
        name="cross_lags",
    )(*receivers, sources, inverse)


def body(n, m, records, taper_select, source_index):
    chans, segs, nwin = records.shape
    nfreq = nwin // 2
    nsrc = source_index.shape[0]
    per = nsrc // n
    share = -(-per // m)
    dft, taper_table, band, inverse, count = make_tables(nwin, nfreq, LAGS)
    me = lax.axis_index("freq")
    mine = lax.axis_index("chan")

    def from_ahead(value, d):
        return lax.ppermute(value, "freq", [(q, (q - d) % n) for q in range(n)])

    def taper_of(select):
        out = jnp.where((select == 0)[:, None], taper_table[0], taper_table[1])
        out = jnp.where((select == 2)[:, None], taper_table[2], out)
        return jnp.where((select == 3)[:, None], taper_table[3], out)

    arrived = []
    for d in range(1, n):
        select = from_ahead(taper_select, d)
        for at in range(0, segs, STEP):
            block = from_ahead(lax.slice_in_dim(records, at, at + STEP, axis=1), d)
            arrived.append((block, select[at : at + STEP]))

    index = jnp.pad(source_index.reshape(n, per), ((0, 0), (0, share * m - per)), constant_values=-1)
    index = index.reshape(n, m, share).transpose(1, 0, 2).reshape(-1)
    rows = index - mine * chans
    owned = (rows >= 0) & (rows < chans) & (index >= 0)
    rows = jnp.clip(rows, 0, chans - 1)
    picked = pick(records, owned.astype(jnp.int32), rows.astype(jnp.int32))
    own_sources = lax.psum_scatter(picked, "chan", scatter_dimension=0, tiled=True)
    own_taper = taper_of(taper_select)
    spectra = whiten_rows(own_sources, own_taper[None], dft, band, count)
    spectra = spectra.reshape(n, share, segs, 2, nfreq).transpose(0, 4, 1, 3, 2)
    pieces = []
    for d in range(n):
        give = lax.dynamic_index_in_dim(spectra, (me - d) % n, 0, keepdims=False)
        pieces.append(from_ahead(give, d) if d else give)
    small = jnp.stack(pieces, axis=3).reshape(nfreq, share, 2 * n * segs)
    gathered = lax.all_gather(small, "chan", axis=1, tiled=True)
    sources = gathered[:, :per]

    receivers = [whiten_across(records, own_taper, dft, band, count)]
    for block, select in arrived:
        receivers.append(whiten_across(block, taper_of(select), dft, band, count))
    return cross_lags(receivers, sources, inverse, 1.0 / math.sqrt(n * segs))


def solution(mesh):
    placed = (P("chan", "freq", None), P("freq"), P())
    return jax.shard_map(
        functools.partial(body, mesh.shape["freq"], mesh.shape["chan"]),
        mesh=mesh,
        in_specs=placed,
        out_specs=P("chan", "freq", None),
        check_vma=False,
    )
```

```python
import functools
import math

import jax
import jax.numpy as jnp
import ml_dtypes
import numpy as np
from jax import lax
from jax.experimental import pallas as pl
from jax.experimental.pallas import tpu as pltpu
from jax.sharding import PartitionSpec as P

LAGS = 256
STEP = 16
F32 = jnp.float32
BF16 = jnp.bfloat16


def make_tables(nwin, nfreq, lags):
    n_int = np.arange(nwin)
    k_int = np.arange(nfreq)
    phase = (n_int[:, None] * k_int[None, :] % nwin) * (2.0 * math.pi / nwin)
    dft = np.concatenate([np.cos(phase), -np.sin(phase)], axis=1) / math.sqrt(nwin)
    sine = np.sin(math.pi * (n_int + 0.5) / nwin)
    taper = np.power(sine[None, :], np.array([0.5, 1.0, 2.0, 3.0])[:, None])
    half = nfreq // 4
    band = np.abs(k_int[:, None] - k_int[None, :]) <= half
    lag_int = np.arange(lags) - lags // 2
    lphase = (k_int[:, None] * lag_int[None, :] % nwin) * (2.0 * math.pi / nwin)
    weight = np.where(k_int == 0, 1.0, 2.0)[:, None] / math.sqrt(2.0 * nfreq)
    inverse = np.concatenate([weight * np.cos(lphase), -weight * np.sin(lphase)], axis=0)
    low = ml_dtypes.bfloat16
    return (
        dft.T.astype(np.float32).astype(low),
        taper.astype(np.float32),
        band.astype(low),
        inverse.T.astype(np.float32).astype(low),
        2 * half + 1,
    )


def pick_kernel(owned_ref, row_ref, x_ref, o_ref):
    def one(s, carry):
        keep = jnp.where(owned_ref[s] == 1, 1.0, 0.0).astype(BF16)
        o_ref[s] = x_ref[row_ref[s]] * keep
        return carry

    lax.fori_loop(0, o_ref.shape[0], one, 0)


def pick(records, owned, rows):
    count = rows.shape[0]
    smem = pl.BlockSpec(memory_space=pltpu.SMEM)
    vmem = pl.BlockSpec(memory_space=pltpu.VMEM)
    return pl.pallas_call(
        pick_kernel,
        out_shape=jax.ShapeDtypeStruct((count,) + records.shape[1:], BF16),
        in_specs=[smem, smem, vmem],
        out_specs=vmem,
        compiler_params=pltpu.CompilerParams(vmem_limit_bytes=40 << 20),
        name="pick",
    )(owned, rows, records)


def whiten_kernel(count, x_ref, t_ref, dft_ref, band_ref, o_ref, xf, of):
    chans, segs, nwin = x_ref.shape
    nfreq = nwin // 2
    lane = 128
    for q in range(nwin // lane):
        cols = slice(q * lane, (q + 1) * lane)
        x = x_ref[:, :, cols].astype(F32) * t_ref[:, cols][None]
        xf[q] = x.reshape(chans * segs, lane)
    for p in range(segs // 2):
        pair = []
        for g in (2 * p, 2 * p + 1):
            parts = [xf[q, pl.ds(g, chans, stride=segs), :] for q in range(nwin // lane)]
            pair.append(jnp.concatenate(parts, axis=1).astype(BF16))
        both = jnp.concatenate(pair, axis=0)
        spectra = lax.dot_general(
            dft_ref[...], both, (((1,), (1,)), ((), ())), preferred_element_type=F32
        )
        real, imag = spectra[:nfreq], spectra[nfreq:]
        power = real * real + imag * imag
        high = power.astype(BF16)
        low = (power - high.astype(F32)).astype(BF16)
        smooth = jnp.dot(band_ref[...], high, preferred_element_type=F32)
        smooth += jnp.dot(band_ref[...], low, preferred_element_type=F32)
        factor = lax.rsqrt(smooth * (1.0 / count) + 1e-06)
        real, imag = real * factor, imag * factor
        for j in range(2):
            cols = slice(j * chans, (j + 1) * chans)
            of[pl.ds(2 * p + j, nfreq, stride=2 * segs), :] = real[:, cols]
            of[pl.ds(segs + 2 * p + j, nfreq, stride=2 * segs), :] = imag[:, cols]
    o_ref[...] = of[...].reshape(nfreq, 2, segs, chans).astype(BF16)


def whiten_across(records, taper, dft, band, count):
    chans, segs, nwin = records.shape
    nfreq = nwin // 2
    return pl.pallas_call(
        functools.partial(whiten_kernel, count),
        out_shape=jax.ShapeDtypeStruct((nfreq, 2, segs, chans), BF16),
        grid=(segs // STEP,),
        in_specs=[
            pl.BlockSpec((chans, STEP, nwin), lambda i: (0, i, 0)),
            pl.BlockSpec((STEP, nwin), lambda i: (i, 0)),
            pl.BlockSpec((nwin, nwin), lambda i: (0, 0)),
            pl.BlockSpec((nfreq, nfreq), lambda i: (0, 0)),
        ],
        out_specs=pl.BlockSpec((nfreq, 2, STEP, chans), lambda i: (0, 0, i, 0)),
        scratch_shapes=[
            pltpu.VMEM((nwin // 128, chans * STEP, 128), F32),
            pltpu.VMEM((nfreq * 2 * STEP, chans), F32),
        ],
        compiler_params=pltpu.CompilerParams(vmem_limit_bytes=48 << 20),
        cost_estimate=pl.CostEstimate(
            flops=4 * chans * segs * nwin * nwin,
            bytes_accessed=4 * chans * segs * nwin,
            transcendentals=0,
        ),
        name="whiten_across",
    )(records, taper, dft, band)


def whiten_rows(block, taper, dft, band, count):
    nfreq = block.shape[-1] // 2
    tapered = (block.astype(F32) * taper).astype(BF16)
    spectra = lax.dot_general(
        tapered, dft, (((tapered.ndim - 1,), (1,)), ((), ())), preferred_element_type=F32
    )
    real, imag = spectra[..., :nfreq], spectra[..., nfreq:]
    power = real * real + imag * imag
    high = power.astype(BF16)
    low = (power - high.astype(F32)).astype(BF16)
    smooth = jnp.dot(high, band, preferred_element_type=F32)
    smooth += jnp.dot(low, band, preferred_element_type=F32)
    factor = lax.rsqrt(smooth / count + 1e-06)
    return jnp.stack([real * factor, imag * factor], axis=-2).astype(BF16)


def cross_kernel(nf, scale, *refs):
    *r_refs, s_ref, inv_ref, o_ref, zs, os = refs
    fb, srcs, depth = s_ref.shape
    nfreq2 = inv_ref.shape[1]
    nfreq = nfreq2 // 2
    chans, group, lags = o_ref.shape
    half = depth // 2
    step = pl.program_id(0)

    @pl.when(step < nf)
    def _():
        for j in range(fb):
            parts = []
            for part in range(2):
                for r in r_refs:
                    parts.append(r[j, part])
            receivers = jnp.concatenate(parts, axis=0)
            s = s_ref[j]
            turned = jnp.concatenate([-s[:, half:], s[:, :half]], axis=1)
            both = jnp.concatenate([s, turned], axis=0)
            cross = jnp.dot(both, receivers, preferred_element_type=F32) * scale
            f = step * fb + j
            zs[pl.ds(f, srcs, stride=nfreq2), :] = cross[:srcs]
            zs[pl.ds(nfreq + f, srcs, stride=nfreq2), :] = cross[srcs:]

    @pl.when(step >= nf)
    def _():
        first = (step - nf) * group
        for p in range(group // 2):
            pair = []
            for t in (2 * p, 2 * p + 1):
                row = pl.multiple_of((first + t) * nfreq2, nfreq2)
                pair.append(zs[pl.ds(row, nfreq2), :].astype(BF16))
            lagged = jnp.dot(
                inv_ref[...], jnp.concatenate(pair, axis=1), preferred_element_type=F32
            )
            turned = lagged.T
            for t in range(2):
                for q in range(lags // 128):
                    os[q, pl.ds(2 * p + t, chans, stride=group), :] = turned[
                        t * chans : (t + 1) * chans, q * 128 : (q + 1) * 128
                    ]
        for q in range(lags // 128):
            o_ref[:, :, q * 128 : (q + 1) * 128] = (
                os[q].reshape(chans, group, 128).astype(BF16)
            )


def cross_lags(receivers, sources, inverse, scale):
    nfreq, srcs, depth = sources.shape
    chans = receivers[0].shape[-1]
    lags = inverse.shape[0]
    fb = 16
    nf = nfreq // fb
    group = min(16, srcs)
    ns = srcs // group
    r_specs = [
        pl.BlockSpec((fb,) + r.shape[1:], lambda i: (jnp.minimum(i, nf - 1), 0, 0, 0))
        for r in receivers
    ]
    return pl.pallas_call(
        functools.partial(cross_kernel, nf, scale),
        out_shape=jax.ShapeDtypeStruct((chans, srcs, lags), BF16),
        grid=(nf + ns,),
        in_specs=r_specs
        + [
            pl.BlockSpec((fb, srcs, depth), lambda i: (jnp.minimum(i, nf - 1), 0, 0)),
            pl.BlockSpec(inverse.shape, lambda i: (0, 0)),
        ],
        out_specs=pl.BlockSpec((chans, group, lags), lambda i: (0, jnp.maximum(i - nf, 0), 0)),
        scratch_shapes=[
            pltpu.VMEM((srcs * 2 * nfreq, chans), F32),
            pltpu.VMEM((lags // 128, chans * group, 128), F32),
        ],
        compiler_params=pltpu.CompilerParams(vmem_limit_bytes=56 << 20),
        name="cross_lags",
    )(*receivers, sources, inverse)


def body(n, m, records, taper_select, source_index):
    chans, segs, nwin = records.shape
    nfreq = nwin // 2
    nsrc = source_index.shape[0]
    per = nsrc // n
    share = -(-per // m)
    dft, taper_table, band, inverse, count = make_tables(nwin, nfreq, LAGS)
    me = lax.axis_index("freq")
    mine = lax.axis_index("chan")

    def from_ahead(value, d):
        return lax.ppermute(value, "freq", [(q, (q - d) % n) for q in range(n)])

    def taper_of(select):
        out = jnp.where((select == 0)[:, None], taper_table[0], taper_table[1])
        out = jnp.where((select == 2)[:, None], taper_table[2], out)
        return jnp.where((select == 3)[:, None], taper_table[3], out)

    arrived = []
    for d in range(1, n):
        select = from_ahead(taper_select, d)
        for at in range(0, segs, STEP):
            block = from_ahead(lax.slice_in_dim(records, at, at + STEP, axis=1), d)
            arrived.append((block, select[at : at + STEP]))

    index = jnp.pad(source_index.reshape(n, per), ((0, 0), (0, share * m - per)), constant_values=-1)
    index = index.reshape(n, m, share).transpose(1, 0, 2).reshape(-1)
    rows = index - mine * chans
    owned = (rows >= 0) & (rows < chans) & (index >= 0)
    rows = jnp.clip(rows, 0, chans - 1)
    picked = pick(records, owned.astype(jnp.int32), rows.astype(jnp.int32))
    own_sources = lax.psum_scatter(picked, "chan", scatter_dimension=0, tiled=True)
    own_taper = taper_of(taper_select)
    receivers = [whiten_across(records, own_taper, dft, band, count)]
    blocks = [block for block, _ in arrived]
    own_sources, receivers, blocks = lax.optimization_barrier((own_sources, receivers, blocks))
    spectra = whiten_rows(own_sources, own_taper[None], dft, band, count)
    spectra = spectra.reshape(n, share, segs, 2, nfreq).transpose(0, 4, 1, 3, 2)
    pieces = []
    for d in range(n):
        give = lax.dynamic_index_in_dim(spectra, (me - d) % n, 0, keepdims=False)
        pieces.append(from_ahead(give, d) if d else give)
    small = jnp.stack(pieces, axis=3).reshape(nfreq, share, 2 * n * segs)
    gathered = lax.all_gather(small, "chan", axis=1, tiled=True)
    sources = gathered[:, :per]

    for block, (_, select) in zip(blocks, arrived):
        receivers.append(whiten_across(block, taper_of(select), dft, band, count))
    return cross_lags(receivers, sources, inverse, 1.0 / math.sqrt(n * segs))


def solution(mesh):
    placed = (P("chan", "freq", None), P("freq"), P())
    return jax.shard_map(
        functools.partial(body, mesh.shape["freq"], mesh.shape["chan"]),
        mesh=mesh,
        in_specs=placed,
        out_specs=P("chan", "freq", None),
        check_vma=False,
    )
```

```python
import functools
import math

import jax
import jax.numpy as jnp
import ml_dtypes
import numpy as np
from jax import lax
from jax.experimental import pallas as pl
from jax.experimental.pallas import tpu as pltpu
from jax.sharding import PartitionSpec as P

LAGS = 256
STEP = 16
F32 = jnp.float32
BF16 = jnp.bfloat16


def make_tables(nwin, nfreq, lags):
    n_int = np.arange(nwin)
    k_int = np.arange(nfreq)
    phase = (n_int[:, None] * k_int[None, :] % nwin) * (2.0 * math.pi / nwin)
    dft = np.concatenate([np.cos(phase), -np.sin(phase)], axis=1) / math.sqrt(nwin)
    sine = np.sin(math.pi * (n_int + 0.5) / nwin)
    taper = np.power(sine[None, :], np.array([0.5, 1.0, 2.0, 3.0])[:, None])
    half = nfreq // 4
    band = np.abs(k_int[:, None] - k_int[None, :]) <= half
    lag_int = np.arange(lags) - lags // 2
    lphase = (k_int[:, None] * lag_int[None, :] % nwin) * (2.0 * math.pi / nwin)
    weight = np.where(k_int == 0, 1.0, 2.0)[:, None] / math.sqrt(2.0 * nfreq)
    inverse = np.concatenate([weight * np.cos(lphase), -weight * np.sin(lphase)], axis=0)
    low = ml_dtypes.bfloat16
    return (
        dft.T.astype(np.float32).astype(low),
        taper.astype(np.float32),
        band.astype(low),
        inverse.T.astype(np.float32).astype(low),
        2 * half + 1,
    )


def pick_kernel(owned_ref, row_ref, x_ref, o_ref):
    def one(s, carry):
        keep = jnp.where(owned_ref[s] == 1, 1.0, 0.0).astype(BF16)
        o_ref[s] = x_ref[row_ref[s]] * keep
        return carry

    lax.fori_loop(0, o_ref.shape[0], one, 0)


def pick(records, owned, rows):
    count = rows.shape[0]
    smem = pl.BlockSpec(memory_space=pltpu.SMEM)
    vmem = pl.BlockSpec(memory_space=pltpu.VMEM)
    return pl.pallas_call(
        pick_kernel,
        out_shape=jax.ShapeDtypeStruct((count,) + records.shape[1:], BF16),
        in_specs=[smem, smem, vmem],
        out_specs=vmem,
        compiler_params=pltpu.CompilerParams(vmem_limit_bytes=40 << 20),
        name="pick",
    )(owned, rows, records)


def whiten_kernel(count, x_ref, t_ref, dft_ref, band_ref, o_ref, xf, of):
    chans, segs, nwin = x_ref.shape
    nfreq = nwin // 2
    lane = 128
    for q in range(nwin // lane):
        cols = slice(q * lane, (q + 1) * lane)
        x = x_ref[:, :, cols].astype(F32) * t_ref[:, cols][None]
        xf[q] = x.reshape(chans * segs, lane)
    for p in range(segs // 2):
        pair = []
        for g in (2 * p, 2 * p + 1):
            parts = [xf[q, pl.ds(g, chans, stride=segs), :] for q in range(nwin // lane)]
            pair.append(jnp.concatenate(parts, axis=1).astype(BF16))
        both = jnp.concatenate(pair, axis=0)
        spectra = lax.dot_general(
            dft_ref[...], both, (((1,), (1,)), ((), ())), preferred_element_type=F32
        )
        real, imag = spectra[:nfreq], spectra[nfreq:]
        power = real * real + imag * imag
        high = power.astype(BF16)
        low = (power - high.astype(F32)).astype(BF16)
        smooth = jnp.dot(band_ref[...], high, preferred_element_type=F32)
        smooth += jnp.dot(band_ref[...], low, preferred_element_type=F32)
        factor = lax.rsqrt(smooth * (1.0 / count) + 1e-06)
        real, imag = real * factor, imag * factor
        for j in range(2):
            cols = slice(j * chans, (j + 1) * chans)
            of[pl.ds(2 * p + j, nfreq, stride=2 * segs), :] = real[:, cols]
            of[pl.ds(segs + 2 * p + j, nfreq, stride=2 * segs), :] = imag[:, cols]
    o_ref[...] = of[...].reshape(nfreq, 2, segs, chans).astype(BF16)


def whiten_across(records, taper, dft, band, count):
    chans, segs, nwin = records.shape
    nfreq = nwin // 2
    return pl.pallas_call(
        functools.partial(whiten_kernel, count),
        out_shape=jax.ShapeDtypeStruct((nfreq, 2, segs, chans), BF16),
        grid=(segs // STEP,),
        in_specs=[
            pl.BlockSpec((chans, STEP, nwin), lambda i: (0, i, 0)),
            pl.BlockSpec((STEP, nwin), lambda i: (i, 0)),
            pl.BlockSpec((nwin, nwin), lambda i: (0, 0)),
            pl.BlockSpec((nfreq, nfreq), lambda i: (0, 0)),
        ],
        out_specs=pl.BlockSpec((nfreq, 2, STEP, chans), lambda i: (0, 0, i, 0)),
        scratch_shapes=[
            pltpu.VMEM((nwin // 128, chans * STEP, 128), F32),
            pltpu.VMEM((nfreq * 2 * STEP, chans), F32),
        ],
        compiler_params=pltpu.CompilerParams(vmem_limit_bytes=48 << 20),
        cost_estimate=pl.CostEstimate(
            flops=4 * chans * segs * nwin * nwin,
            bytes_accessed=4 * chans * segs * nwin,
            transcendentals=0,
        ),
        name="whiten_across",
    )(records, taper, dft, band)


def whiten_rows(block, taper, dft, band, count):
    nfreq = block.shape[-1] // 2
    tapered = (block.astype(F32) * taper).astype(BF16)
    spectra = lax.dot_general(
        tapered, dft, (((tapered.ndim - 1,), (1,)), ((), ())), preferred_element_type=F32
    )
    real, imag = spectra[..., :nfreq], spectra[..., nfreq:]
    power = real * real + imag * imag
    high = power.astype(BF16)
    low = (power - high.astype(F32)).astype(BF16)
    smooth = jnp.dot(high, band, preferred_element_type=F32)
    smooth += jnp.dot(low, band, preferred_element_type=F32)
    factor = lax.rsqrt(smooth / count + 1e-06)
    return jnp.stack([real * factor, imag * factor], axis=-2).astype(BF16)


def cross_kernel(nf, scale, *refs):
    *r_refs, s_ref, inv_ref, o_ref, zs, os = refs
    fb, srcs, depth = s_ref.shape
    nfreq2 = inv_ref.shape[1]
    nfreq = nfreq2 // 2
    chans, group, lags = o_ref.shape
    half = depth // 2
    step = pl.program_id(0)

    @pl.when(step < nf)
    def _():
        for j in range(fb):
            parts = []
            for part in range(2):
                for r in r_refs:
                    parts.append(r[j, part])
            receivers = jnp.concatenate(parts, axis=0)
            s = s_ref[j]
            turned = jnp.concatenate([-s[:, half:], s[:, :half]], axis=1)
            both = jnp.concatenate([s, turned], axis=0)
            cross = jnp.dot(both, receivers, preferred_element_type=F32) * scale
            f = step * fb + j
            zs[pl.ds(f, srcs, stride=nfreq2), :] = cross[:srcs]
            zs[pl.ds(nfreq + f, srcs, stride=nfreq2), :] = cross[srcs:]

    @pl.when(step >= nf)
    def _():
        first = (step - nf) * group
        for p in range(group // 2):
            pair = []
            for t in (2 * p, 2 * p + 1):
                row = pl.multiple_of((first + t) * nfreq2, nfreq2)
                pair.append(zs[pl.ds(row, nfreq2), :].astype(BF16))
            lagged = jnp.dot(
                inv_ref[...], jnp.concatenate(pair, axis=1), preferred_element_type=F32
            )
            turned = lagged.T
            for t in range(2):
                for q in range(lags // 128):
                    os[q, pl.ds(2 * p + t, chans, stride=group), :] = turned[
                        t * chans : (t + 1) * chans, q * 128 : (q + 1) * 128
                    ]
        for q in range(lags // 128):
            o_ref[:, :, q * 128 : (q + 1) * 128] = (
                os[q].reshape(chans, group, 128).astype(BF16)
            )


def cross_lags(receivers, sources, inverse, scale):
    nfreq, srcs, depth = sources.shape
    chans = receivers[0].shape[-1]
    lags = inverse.shape[0]
    fb = 16
    nf = nfreq // fb
    group = min(16, srcs)
    ns = srcs // group
    r_specs = [
        pl.BlockSpec((fb,) + r.shape[1:], lambda i: (jnp.minimum(i, nf - 1), 0, 0, 0))
        for r in receivers
    ]
    return pl.pallas_call(
        functools.partial(cross_kernel, nf, scale),
        out_shape=jax.ShapeDtypeStruct((chans, srcs, lags), BF16),
        grid=(nf + ns,),
        in_specs=r_specs
        + [
            pl.BlockSpec((fb, srcs, depth), lambda i: (jnp.minimum(i, nf - 1), 0, 0)),
            pl.BlockSpec(inverse.shape, lambda i: (0, 0)),
        ],
        out_specs=pl.BlockSpec((chans, group, lags), lambda i: (0, jnp.maximum(i - nf, 0), 0)),
        scratch_shapes=[
            pltpu.VMEM((srcs * 2 * nfreq, chans), F32),
            pltpu.VMEM((lags // 128, chans * group, 128), F32),
        ],
        compiler_params=pltpu.CompilerParams(vmem_limit_bytes=56 << 20),
        name="cross_lags",
    )(*receivers, sources, inverse)


def body(n, m, records, taper_select, source_index):
    chans, segs, nwin = records.shape
    nfreq = nwin // 2
    nsrc = source_index.shape[0]
    per = nsrc // n
    share = -(-per // m)
    dft, taper_table, band, inverse, count = make_tables(nwin, nfreq, LAGS)
    me = lax.axis_index("freq")
    mine = lax.axis_index("chan")

    def from_ahead(value, d):
        return lax.ppermute(value, "freq", [(q, (q - d) % n) for q in range(n)])

    def taper_of(select):
        out = jnp.where((select == 0)[:, None], taper_table[0], taper_table[1])
        out = jnp.where((select == 2)[:, None], taper_table[2], out)
        return jnp.where((select == 3)[:, None], taper_table[3], out)

    arrived = []
    for d in range(1, n):
        select = from_ahead(taper_select, d)
        for at in range(0, segs, STEP):
            block = from_ahead(lax.slice_in_dim(records, at, at + STEP, axis=1), d)
            arrived.append((block, select[at : at + STEP]))

    index = jnp.pad(source_index.reshape(n, per), ((0, 0), (0, share * m - per)), constant_values=-1)
    index = index.reshape(n, 2, m // 2, share).transpose(1, 2, 0, 3).reshape(2, -1)
    side = lax.rem(mine, 2)
    groups = [list(range(c, m, 2)) for c in range(2)]
    swap = [(q, q ^ 1) for q in range(m)]

    def pick_for(index):
        rows = index - mine * chans
        owned = (rows >= 0) & (rows < chans) & (index >= 0)
        rows = jnp.clip(rows, 0, chans - 1)
        return pick(records, owned.astype(jnp.int32), rows.astype(jnp.int32))

    given = pick_for(jnp.where(side == 0, index[1], index[0]))
    given = lax.ppermute(given, "chan", swap)
    picked = pick_for(jnp.where(side == 0, index[0], index[1])) + given
    own_sources = lax.psum_scatter(
        picked, "chan", scatter_dimension=0, axis_index_groups=groups, tiled=True
    )
    own_taper = taper_of(taper_select)
    receivers = [whiten_across(records, own_taper, dft, band, count)]
    blocks = [block for block, _ in arrived]
    early = blocks[: len(blocks) // 2]
    own_sources, receivers, early = lax.optimization_barrier((own_sources, receivers, early))
    blocks = early + blocks[len(blocks) // 2 :]
    spectra = whiten_rows(own_sources, own_taper[None], dft, band, count)
    spectra = spectra.reshape(n, share, segs, 2, nfreq).transpose(0, 4, 1, 3, 2)
    pieces = []
    for d in range(n):
        give = lax.dynamic_index_in_dim(spectra, (me - d) % n, 0, keepdims=False)
        pieces.append(from_ahead(give, d) if d else give)
    small = jnp.stack(pieces, axis=3).reshape(nfreq, share, 2 * n * segs)
    gathered = lax.all_gather(small, "chan", axis=1, axis_index_groups=groups, tiled=True)
    other = lax.ppermute(gathered, "chan", swap)
    first = jnp.where(side == 0, gathered, other)
    second = jnp.where(side == 0, other, gathered)
    sources = jnp.concatenate([first, second], axis=1)[:, :per]

    for block, (_, select) in zip(blocks, arrived):
        receivers.append(whiten_across(block, taper_of(select), dft, band, count))
    return cross_lags(receivers, sources, inverse, 1.0 / math.sqrt(n * segs))


def solution(mesh):
    placed = (P("chan", "freq", None), P("freq"), P())
    return jax.shard_map(
        functools.partial(body, mesh.shape["freq"], mesh.shape["chan"]),
        mesh=mesh,
        in_specs=placed,
        out_specs=P("chan", "freq", None),
        check_vma=False,
    )
```

```python
import functools
import math

import jax
import jax.numpy as jnp
import ml_dtypes
import numpy as np
from jax import lax
from jax.experimental import pallas as pl
from jax.experimental.pallas import tpu as pltpu
from jax.sharding import PartitionSpec as P

LAGS = 256
STEP = 16
F32 = jnp.float32
BF16 = jnp.bfloat16


def make_tables(nwin, nfreq, lags):
    n_int = np.arange(nwin)
    k_int = np.arange(nfreq)
    phase = (n_int[:, None] * k_int[None, :] % nwin) * (2.0 * math.pi / nwin)
    dft = np.concatenate([np.cos(phase), -np.sin(phase)], axis=1) / math.sqrt(nwin)
    sine = np.sin(math.pi * (n_int + 0.5) / nwin)
    taper = np.power(sine[None, :], np.array([0.5, 1.0, 2.0, 3.0])[:, None])
    half = nfreq // 4
    band = np.abs(k_int[:, None] - k_int[None, :]) <= half
    lag_int = np.arange(lags) - lags // 2
    lphase = (k_int[:, None] * lag_int[None, :] % nwin) * (2.0 * math.pi / nwin)
    weight = np.where(k_int == 0, 1.0, 2.0)[:, None] / math.sqrt(2.0 * nfreq)
    inverse = np.concatenate([weight * np.cos(lphase), -weight * np.sin(lphase)], axis=0)
    low = ml_dtypes.bfloat16
    return (
        dft.T.astype(np.float32).astype(low),
        taper.astype(np.float32),
        band.astype(low),
        inverse.T.astype(np.float32).astype(low),
        2 * half + 1,
    )


def pick_kernel(owned_ref, row_ref, x_ref, o_ref):
    def one(s, carry):
        keep = jnp.where(owned_ref[s] == 1, 1.0, 0.0).astype(BF16)
        o_ref[s] = x_ref[row_ref[s]] * keep
        return carry

    lax.fori_loop(0, o_ref.shape[0], one, 0)


def pick(records, owned, rows):
    count = rows.shape[0]
    smem = pl.BlockSpec(memory_space=pltpu.SMEM)
    vmem = pl.BlockSpec(memory_space=pltpu.VMEM)
    return pl.pallas_call(
        pick_kernel,
        out_shape=jax.ShapeDtypeStruct((count,) + records.shape[1:], BF16),
        in_specs=[smem, smem, vmem],
        out_specs=vmem,
        compiler_params=pltpu.CompilerParams(vmem_limit_bytes=40 << 20),
        name="pick",
    )(owned, rows, records)


def whiten_kernel(count, x_ref, t_ref, dft_ref, band_ref, o_ref, xf, of):
    chans, segs, nwin = x_ref.shape
    nfreq = nwin // 2
    lane = 128
    for q in range(nwin // lane):
        cols = slice(q * lane, (q + 1) * lane)
        x = x_ref[:, :, cols].astype(F32) * t_ref[:, cols][None]
        xf[q] = x.reshape(chans * segs, lane)
    for p in range(segs // 2):
        pair = []
        for g in (2 * p, 2 * p + 1):
            parts = [xf[q, pl.ds(g, chans, stride=segs), :] for q in range(nwin // lane)]
            pair.append(jnp.concatenate(parts, axis=1).astype(BF16))
        both = jnp.concatenate(pair, axis=0)
        spectra = lax.dot_general(
            dft_ref[...], both, (((1,), (1,)), ((), ())), preferred_element_type=F32
        )
        real, imag = spectra[:nfreq], spectra[nfreq:]
        power = real * real + imag * imag
        high = power.astype(BF16)
        low = (power - high.astype(F32)).astype(BF16)
        smooth = jnp.dot(band_ref[...], high, preferred_element_type=F32)
        smooth += jnp.dot(band_ref[...], low, preferred_element_type=F32)
        factor = lax.rsqrt(smooth * (1.0 / count) + 1e-06)
        real, imag = real * factor, imag * factor
        for j in range(2):
            cols = slice(j * chans, (j + 1) * chans)
            of[pl.ds(2 * p + j, nfreq, stride=2 * segs), :] = real[:, cols]
            of[pl.ds(segs + 2 * p + j, nfreq, stride=2 * segs), :] = imag[:, cols]
    o_ref[...] = of[...].reshape(nfreq, 2, segs, chans).astype(BF16)


def whiten_across(records, taper, dft, band, count):
    chans, segs, nwin = records.shape
    nfreq = nwin // 2
    return pl.pallas_call(
        functools.partial(whiten_kernel, count),
        out_shape=jax.ShapeDtypeStruct((nfreq, 2, segs, chans), BF16),
        grid=(segs // STEP,),
        in_specs=[
            pl.BlockSpec((chans, STEP, nwin), lambda i: (0, i, 0)),
            pl.BlockSpec((STEP, nwin), lambda i: (i, 0)),
            pl.BlockSpec((nwin, nwin), lambda i: (0, 0)),
            pl.BlockSpec((nfreq, nfreq), lambda i: (0, 0)),
        ],
        out_specs=pl.BlockSpec((nfreq, 2, STEP, chans), lambda i: (0, 0, i, 0)),
        scratch_shapes=[
            pltpu.VMEM((nwin // 128, chans * STEP, 128), F32),
            pltpu.VMEM((nfreq * 2 * STEP, chans), F32),
        ],
        compiler_params=pltpu.CompilerParams(vmem_limit_bytes=48 << 20),
        cost_estimate=pl.CostEstimate(
            flops=4 * chans * segs * nwin * nwin,
            bytes_accessed=4 * chans * segs * nwin,
            transcendentals=0,
        ),
        name="whiten_across",
    )(records, taper, dft, band)


def whiten_rows(block, taper, dft, band, count):
    nfreq = block.shape[-1] // 2
    tapered = (block.astype(F32) * taper).astype(BF16)
    spectra = lax.dot_general(
        tapered, dft, (((tapered.ndim - 1,), (1,)), ((), ())), preferred_element_type=F32
    )
    real, imag = spectra[..., :nfreq], spectra[..., nfreq:]
    power = real * real + imag * imag
    high = power.astype(BF16)
    low = (power - high.astype(F32)).astype(BF16)
    smooth = jnp.dot(high, band, preferred_element_type=F32)
    smooth += jnp.dot(low, band, preferred_element_type=F32)
    factor = lax.rsqrt(smooth / count + 1e-06)
    return jnp.stack([real * factor, imag * factor], axis=-2).astype(BF16)


def cross_kernel(nf, scale, *refs):
    *r_refs, s_ref, inv_ref, o_ref, zs, os = refs
    fb, srcs, depth = s_ref.shape
    nfreq2 = inv_ref.shape[1]
    nfreq = nfreq2 // 2
    chans, group, lags = o_ref.shape
    half = depth // 2
    step = pl.program_id(0)

    @pl.when(step < nf)
    def _():
        for j in range(fb):
            parts = []
            for part in range(2):
                for r in r_refs:
                    parts.append(r[j, part])
            receivers = jnp.concatenate(parts, axis=0)
            s = s_ref[j]
            turned = jnp.concatenate([-s[:, half:], s[:, :half]], axis=1)
            both = jnp.concatenate([s, turned], axis=0)
            cross = jnp.dot(both, receivers, preferred_element_type=F32) * scale
            f = step * fb + j
            zs[pl.ds(f, srcs, stride=nfreq2), :] = cross[:srcs]
            zs[pl.ds(nfreq + f, srcs, stride=nfreq2), :] = cross[srcs:]

    @pl.when(step >= nf)
    def _():
        first = (step - nf) * group
        for p in range(group // 2):
            pair = []
            for t in (2 * p, 2 * p + 1):
                row = pl.multiple_of((first + t) * nfreq2, nfreq2)
                pair.append(zs[pl.ds(row, nfreq2), :].astype(BF16))
            lagged = jnp.dot(
                inv_ref[...], jnp.concatenate(pair, axis=1), preferred_element_type=F32
            )
            turned = lagged.T
            for t in range(2):
                for q in range(lags // 128):
                    os[q, pl.ds(2 * p + t, chans, stride=group), :] = turned[
                        t * chans : (t + 1) * chans, q * 128 : (q + 1) * 128
                    ]
        for q in range(lags // 128):
            o_ref[:, :, q * 128 : (q + 1) * 128] = (
                os[q].reshape(chans, group, 128).astype(BF16)
            )


def cross_lags(receivers, sources, inverse, scale):
    nfreq, srcs, depth = sources.shape
    chans = receivers[0].shape[-1]
    lags = inverse.shape[0]
    fb = 16
    nf = nfreq // fb
    group = min(16, srcs)
    ns = srcs // group
    r_specs = [
        pl.BlockSpec((fb,) + r.shape[1:], lambda i: (jnp.minimum(i, nf - 1), 0, 0, 0))
        for r in receivers
    ]
    return pl.pallas_call(
        functools.partial(cross_kernel, nf, scale),
        out_shape=jax.ShapeDtypeStruct((chans, srcs, lags), BF16),
        grid=(nf + ns,),
        in_specs=r_specs
        + [
            pl.BlockSpec((fb, srcs, depth), lambda i: (jnp.minimum(i, nf - 1), 0, 0)),
            pl.BlockSpec(inverse.shape, lambda i: (0, 0)),
        ],
        out_specs=pl.BlockSpec((chans, group, lags), lambda i: (0, jnp.maximum(i - nf, 0), 0)),
        scratch_shapes=[
            pltpu.VMEM((srcs * 2 * nfreq, chans), F32),
            pltpu.VMEM((lags // 128, chans * group, 128), F32),
        ],
        compiler_params=pltpu.CompilerParams(vmem_limit_bytes=56 << 20),
        name="cross_lags",
    )(*receivers, sources, inverse)


def body(n, m, records, taper_select, source_index):
    chans, segs, nwin = records.shape
    nfreq = nwin // 2
    nsrc = source_index.shape[0]
    per = nsrc // n
    share = -(-per // m)
    dft, taper_table, band, inverse, count = make_tables(nwin, nfreq, LAGS)
    me = lax.axis_index("freq")
    mine = lax.axis_index("chan")

    def from_ahead(value, d):
        return lax.ppermute(value, "freq", [(q, (q - d) % n) for q in range(n)])

    def taper_of(select):
        out = jnp.where((select == 0)[:, None], taper_table[0], taper_table[1])
        out = jnp.where((select == 2)[:, None], taper_table[2], out)
        return jnp.where((select == 3)[:, None], taper_table[3], out)

    arrived = []
    for d in range(1, n):
        select = from_ahead(taper_select, d)
        for at in range(0, segs, STEP):
            block = from_ahead(lax.slice_in_dim(records, at, at + STEP, axis=1), d)
            arrived.append((block, select[at : at + STEP]))

    index = jnp.pad(source_index.reshape(n, per), ((0, 0), (0, share * m - per)), constant_values=-1)
    index = index.reshape(n, 2, m // 2, share).transpose(1, 2, 0, 3).reshape(2, -1)
    side = lax.rem(mine, 2)
    groups = [list(range(c, m, 2)) for c in range(2)]
    swap = [(q, q ^ 1) for q in range(m)]

    def pick_for(index):
        rows = index - mine * chans
        owned = (rows >= 0) & (rows < chans) & (index >= 0)
        rows = jnp.clip(rows, 0, chans - 1)
        return pick(records, owned.astype(jnp.int32), rows.astype(jnp.int32))

    given = pick_for(jnp.where(side == 0, index[1], index[0]))
    given = lax.ppermute(given, "chan", swap)
    picked = pick_for(jnp.where(side == 0, index[0], index[1])) + given
    own_sources = lax.psum_scatter(
        picked, "chan", scatter_dimension=0, axis_index_groups=groups, tiled=True
    )
    own_taper = taper_of(taper_select)
    receivers = [whiten_across(records, own_taper, dft, band, count)]
    blocks = [block for block, _ in arrived]
    early = blocks[: len(blocks) // 2]
    own_sources, receivers, early = lax.optimization_barrier((own_sources, receivers, early))
    blocks = early + blocks[len(blocks) // 2 :]
    spectra = whiten_rows(own_sources, own_taper[None], dft, band, count)
    spectra = spectra.reshape(n, share, segs, 2, nfreq).transpose(0, 4, 1, 3, 2)
    pieces = []
    for d in range(n):
        give = lax.dynamic_index_in_dim(spectra, (me - d) % n, 0, keepdims=False)
        pieces.append(from_ahead(give, d) if d else give)
    small = jnp.stack(pieces, axis=3).reshape(nfreq, share, 2 * n * segs)
    gathered = lax.all_gather(small, "chan", axis=1, axis_index_groups=groups, tiled=True)
    for block, (_, select) in zip(blocks, arrived):
        receivers.append(whiten_across(block, taper_of(select), dft, band, count))
    gathered, receivers = lax.optimization_barrier((gathered, receivers))
    other = lax.ppermute(gathered, "chan", swap)
    first = jnp.where(side == 0, gathered, other)
    second = jnp.where(side == 0, other, gathered)
    sources = jnp.concatenate([first, second], axis=1)[:, :per]

    return cross_lags(receivers, sources, inverse, 1.0 / math.sqrt(n * segs))


def solution(mesh):
    placed = (P("chan", "freq", None), P("freq"), P())
    return jax.shard_map(
        functools.partial(body, mesh.shape["freq"], mesh.shape["chan"]),
        mesh=mesh,
        in_specs=placed,
        out_specs=P("chan", "freq", None),
        check_vma=False,
    )
```
